512 devices in a mesh: row: 16 (over x_lo, y), col: 32 (over z, x_hi, core).
Axes of the slice: x: 4 (x_hi: 2, x_lo: 2; x = x_hi * 2 + x_lo), y: 8, z: 8, core: 2. Of those that a mesh axis runs over, the one named last changes fastest.
Arguments:
- inputs: bfloat16 [512, 12288], P('col', 'row'), may hold values from -6 to 6
- w_up: bfloat16 [12288, 24576], P('row', 'col'), may hold values from -0.0546875 to 0.0546875
- w_down: bfloat16 [24576, 12288], P('col', 'row'), may hold values from -0.0390625 to 0.0390625
- grad_out: bfloat16 [512, 12288], P('col', 'row'), may hold values from -1.5 to 1.5
Outputs:
- grad_in: bfloat16 [512, 12288], P('col', 'row')
- grad_up: bfloat16 [12288, 24576], P('row', 'col')
- grad_down: bfloat16 [24576, 12288], P('col', 'row')
The draws below stay inside these ranges and needn't reach their ends.
All inputs are finite; a program needn't handle non-finite values.
Results may differ from the reference program's by a relative error of at most 0.0049.
Values may be sent and summed in bfloat16 or wider, within the bound.
No kernel may reach another device: no remote copies, remote signals or barrier semaphores. Data moves between devices by JAX's collectives and lax.ppermute only.
A program may use at most 64 MiB of HBM per device.

```python
import math
import jax
import jax.numpy as jnp
from jax import lax

D = 12288
FF = 24576
TOKENS = 512


def level_of(stream_key, shape, pieces, smallest, high):
    factor_of = 1.0
    for dim, blocks in pieces:
        heights = jax.random.uniform(jax.random.fold_in(jax.random.fold_in(stream_key, 6), dim), (blocks,), jnp.float32, smallest / len(pieces), high / len(pieces))
        factor_of = factor_of * jnp.repeat(jnp.exp(heights), shape[dim] // blocks).reshape((-1,) + (1,) * (len(shape) - 1 - dim))
    return factor_of


def scatter_about(rng, dims, spread, most, shards=(), kind=jnp.bfloat16):
    entries = jax.random.normal(rng, dims, jnp.float32) * spread
    if len(shards) > 0:
        entries = level_of(rng, dims, shards, -0.22, 0.18) * entries
    return jnp.clip(entries, min=-most, max=most).astype(kind)


def setup_inputs(seed: int = 0) -> dict:
    splits = jax.random.split(jax.random.key(seed), 5)
    inputs = scatter_about(splits[0], (TOKENS, D), 1.0, 6.0, ((0, 32), (1, 16)))
    w_up = scatter_about(splits[1], (D, FF), D ** -0.5, 0.0546875, ((0, 16), (1, 32)))
    w_down = scatter_about(splits[2], (FF, D), FF ** -0.5, 0.0390625, ((0, 32), (1, 16)))
    grad_out = scatter_about(splits[3], (TOKENS, D), 0.25, 1.5, ((0, 32), (1, 16)))
    return dict(inputs=inputs, w_up=w_up, w_down=w_down, grad_out=grad_out)


gelu_scale = math.sqrt(2.0 / math.pi)
cubic_coef = 0.044715

def gelu_parts(pre_act):
    tangent = jnp.tanh(gelu_scale * (pre_act + cubic_coef * pre_act * pre_act * pre_act))
    gelu_value = 0.5 * pre_act * (1.0 + tangent)
    gelu_slope = 0.5 * (1.0 + tangent) + 0.5 * pre_act * (1.0 - tangent * tangent) * gelu_scale * (1.0 + 3.0 * cubic_coef * pre_act * pre_act)
    return (gelu_value, gelu_slope)

def reference(inputs, w_up, w_down, grad_out):
    pre_act = jnp.dot(inputs, w_up, preferred_element_type=jnp.float32)
    gelu_value, gelu_slope = gelu_parts(pre_act)
    act = gelu_value.astype(jnp.bfloat16)
    grad_act = lax.dot_general(grad_out, w_down, (((1,), (1,)), ((), ())), preferred_element_type=jnp.float32)
    grad_pre = (grad_act * gelu_slope).astype(jnp.bfloat16)
    grad_up = lax.dot_general(inputs, grad_pre, (((0,), (0,)), ((), ())), preferred_element_type=jnp.float32)
    grad_down = lax.dot_general(act, grad_out, (((0,), (0,)), ((), ())), preferred_element_type=jnp.float32)
    grad_in = lax.dot_general(grad_pre, w_up, (((1,), (1,)), ((), ())), preferred_element_type=jnp.float32)
    return (grad_in.astype(jnp.bfloat16), grad_up.astype(jnp.bfloat16), grad_down.astype(jnp.bfloat16))
```

```python
import math

import jax
import jax.numpy as jnp
from jax import lax
from jax.sharding import Mesh, PartitionSpec as P

gelu_scale = math.sqrt(2.0 / math.pi)
cubic_coef = 0.044715


def gelu_parts(pre_act):
    tangent = jnp.tanh(gelu_scale * (pre_act + cubic_coef * pre_act * pre_act * pre_act))
    gelu_value = 0.5 * pre_act * (1.0 + tangent)
    gelu_slope = 0.5 * (1.0 + tangent) + 0.5 * pre_act * (1.0 - tangent * tangent) * gelu_scale * (
        1.0 + 3.0 * cubic_coef * pre_act * pre_act
    )
    return (gelu_value, gelu_slope)


ROW = ("xl", "y")


def swap(blocks, axes):
    return lax.all_to_all(blocks, axes, split_axis=0, concat_axis=0, tiled=True)


def spread(block, axes, size):
    copies = jnp.broadcast_to(block[None], (size,) + block.shape)
    return swap(copies.reshape((size * block.shape[0],) + block.shape[1:]), axes)


def per_device(inputs, w_up, w_down, grad_out):
    f32, bf16 = jnp.float32, jnp.bfloat16
    tokens, width = inputs.shape
    hidden = w_up.shape[1]
    both = spread(jnp.concatenate([inputs, grad_out], axis=0), "z", 8)
    both = lax.all_gather(both, "xh", axis=0, tiled=True).reshape(16, 2, tokens, width)
    whole_in = lax.all_gather(both[:, 0].reshape(-1, width), "c", axis=0, tiled=True)
    whole_grad = lax.all_gather(both[:, 1].reshape(-1, width), "c", axis=0, tiled=True)

    pre_term = jnp.dot(whole_in, w_up, preferred_element_type=f32).astype(bf16)
    back_term = lax.dot_general(
        whole_grad, w_down, (((1,), (1,)), ((), ())), preferred_element_type=f32
    ).astype(bf16)
    terms = jnp.stack(
        [pre_term.reshape(16, -1, hidden), back_term.reshape(16, -1, hidden)], axis=1
    )
    terms = swap(terms.reshape(-1, hidden), ROW).reshape(16, 2, -1, hidden)
    sums = jnp.sum(terms.astype(f32), axis=0)
    gelu_value, gelu_slope = gelu_parts(sums[0])
    mine = jnp.concatenate(
        [gelu_value.astype(bf16), (sums[1] * gelu_slope).astype(bf16)], axis=0
    )
    full = spread(mine, ROW, 16).reshape(16, 2, -1, hidden)
    act, dpre = full[:, 0].reshape(-1, hidden), full[:, 1].reshape(-1, hidden)

    partial_in = lax.dot_general(
        dpre, w_up, (((1,), (1,)), ((), ())), preferred_element_type=f32
    )
    halves = swap(partial_in, "c").reshape(2, -1, width)
    halves = (halves[0] + halves[1]).astype(bf16)
    pieces = swap(halves, ("xh", "z")).reshape(16, -1, width)
    grad_in = jnp.sum(pieces.astype(f32), axis=0).astype(bf16)

    grad_up = lax.dot_general(
        whole_in, dpre, (((0,), (0,)), ((), ())), preferred_element_type=f32
    )
    grad_down = lax.dot_general(
        act, whole_grad, (((0,), (0,)), ((), ())), preferred_element_type=f32
    )
    return (grad_in, grad_up.astype(bf16), grad_down.astype(bf16))


def solution(mesh):
    fine = Mesh(mesh.devices.reshape(2, 8, 8, 2, 2), ("xl", "y", "z", "xh", "c"))
    row, col = ("xl", "y"), ("z", "xh", "c")
    in_specs = (P(col, row), P(row, col), P(col, row), P(col, row))
    out_specs = (P(col, row), P(row, col), P(col, row))
    return jax.shard_map(
        per_device, mesh=fine, in_specs=in_specs, out_specs=out_specs, check_vma=False
    )
```

```python
import math

import jax
import jax.numpy as jnp
from jax import lax
from jax.sharding import Mesh, PartitionSpec as P

gelu_scale = math.sqrt(2.0 / math.pi)
cubic_coef = 0.044715


def gelu_parts(pre_act):
    tangent = jnp.tanh(gelu_scale * (pre_act + cubic_coef * pre_act * pre_act * pre_act))
    gelu_value = 0.5 * pre_act * (1.0 + tangent)
    gelu_slope = 0.5 * (1.0 + tangent) + 0.5 * pre_act * (1.0 - tangent * tangent) * gelu_scale * (
        1.0 + 3.0 * cubic_coef * pre_act * pre_act
    )
    return (gelu_value, gelu_slope)


def swap(blocks, axes):
    return lax.all_to_all(blocks, axes, split_axis=0, concat_axis=0, tiled=True)


def spread(block, axes, size):
    copies = jnp.broadcast_to(block[None], (size,) + block.shape)
    return swap(copies.reshape((size * block.shape[0],) + block.shape[1:]), axes)


def gather(block, axis):
    return lax.all_gather(block, axis, axis=0, tiled=True)


def other(block, axis):
    return lax.ppermute(block, axis, [(0, 1), (1, 0)])


def per_device(inputs, w_up, w_down, grad_out):
    f32, bf16 = jnp.float32, jnp.bfloat16
    tokens, width = inputs.shape
    hidden = w_up.shape[1]
    xl, xh, core = lax.axis_index("xl"), lax.axis_index("xh"), lax.axis_index("c")

    def over_cores(part):
        part = gather(part, "c").reshape(16, 2, tokens, width)
        return part[:, 0].reshape(-1, width), part[:, 1].reshape(-1, width)

    def half(rows, which):
        size = rows.shape[0] // 2
        return lax.dynamic_slice_in_dim(rows, which * size, size, 0)

    def pre_and_back(whole_in, whole_grad, which):
        return jnp.stack(
            [
                jnp.dot(half(whole_in, which), w_up, preferred_element_type=f32),
                lax.dot_general(
                    half(whole_grad, which),
                    w_down,
                    (((1,), (1,)), ((), ())),
                    preferred_element_type=f32,
                ),
            ]
        )

    def pair_sums(whole_in, whole_grad):
        got = other(pre_and_back(whole_in, whole_grad, 1 - xl).astype(bf16), "xl")
        sums = pre_and_back(whole_in, whole_grad, xl) + got.astype(f32)
        return sums.astype(bf16).reshape(2, 8, tokens, hidden)

    def row_sums(pairs):
        pieces = swap(jnp.swapaxes(pairs, 0, 1).reshape(-1, hidden), "y")
        return jnp.sum(pieces.reshape(8, 2, tokens, hidden).astype(f32), axis=0)

    near = spread(jnp.concatenate([inputs, grad_out], axis=0), "z", 8)
    far = other(near, "xh")
    near_in, near_grad = over_cores(near)
    near_sums = row_sums(pair_sums(near_in, near_grad))
    far_in, far_grad = over_cores(far)
    far_sums = row_sums(pair_sums(far_in, far_grad))

    pre = jnp.concatenate([near_sums[0], far_sums[0]], axis=0)
    back = jnp.concatenate([near_sums[1], far_sums[1]], axis=0)
    gelu_value, gelu_slope = gelu_parts(pre)
    dpre_mine = spread((back * gelu_slope).astype(bf16), "y", 8)
    dpre_mine, act_rows = lax.optimization_barrier((dpre_mine, gelu_value.astype(bf16)))
    dpre_other = other(dpre_mine, "xl")
    act_mine = spread(act_rows, "y", 8)

    def in_of(rows):
        return lax.dot_general(
            rows, w_up, (((1,), (1,)), ((), ())), preferred_element_type=f32
        )

    from_mine, from_other = in_of(dpre_mine), in_of(dpre_other)
    same = core == xl
    kept = jnp.where(same, from_mine, from_other)
    given = jnp.where(same, from_other, from_mine)
    given, act_mine = lax.optimization_barrier((given, act_mine))
    act_other = other(act_mine, "xl")
    kept = (kept + other(given, "c")).astype(bf16).reshape(8, 2, tokens, width)
    first = xh == 0
    kept = jnp.stack(
        [
            jnp.where(first, kept[:, 0], kept[:, 1]),
            jnp.where(first, kept[:, 1], kept[:, 0]),
        ]
    ).reshape(-1, width)
    pieces = swap(kept, ("xh", "z")).reshape(16, tokens, width)
    grad_in = jnp.sum(pieces.astype(f32), axis=0).astype(bf16)

    def by_half(near, far):
        rows = [x.reshape(2, 8, tokens, width) for x in (near, far)]
        rows = jnp.stack(rows, axis=2).reshape(2, -1, width)
        return (
            lax.dynamic_index_in_dim(rows, xl, 0, False),
            lax.dynamic_index_in_dim(rows, 1 - xl, 0, False),
        )

    def over_tokens(left, right):
        return lax.dot_general(
            left, right, (((0,), (0,)), ((), ())), preferred_element_type=f32
        )

    in_mine, in_other = by_half(near_in, far_in)
    grad_mine, grad_other = by_half(near_grad, far_grad)
    grad_up = over_tokens(in_mine, dpre_mine) + over_tokens(in_other, dpre_other)
    grad_down = over_tokens(act_mine, grad_mine) + over_tokens(act_other, grad_other)
    return (grad_in, grad_up.astype(bf16), grad_down.astype(bf16))


def solution(mesh):
    fine = Mesh(mesh.devices.reshape(2, 8, 8, 2, 2), ("xl", "y", "z", "xh", "c"))
    row, col = ("xl", "y"), ("z", "xh", "c")
    in_specs = (P(col, row), P(row, col), P(col, row), P(col, row))
    out_specs = (P(col, row), P(row, col), P(col, row))
    return jax.shard_map(
        per_device, mesh=fine, in_specs=in_specs, out_specs=out_specs, check_vma=False
    )
```

```python
import math

import jax
import jax.numpy as jnp
from jax import lax
from jax.sharding import Mesh, PartitionSpec as P

gelu_scale = math.sqrt(2.0 / math.pi)
cubic_coef = 0.044715


def gelu_parts(pre_act):
    tangent = jnp.tanh(gelu_scale * (pre_act + cubic_coef * pre_act * pre_act * pre_act))
    gelu_value = 0.5 * pre_act * (1.0 + tangent)
    gelu_slope = 0.5 * (1.0 + tangent) + 0.5 * pre_act * (1.0 - tangent * tangent) * gelu_scale * (
        1.0 + 3.0 * cubic_coef * pre_act * pre_act
    )
    return (gelu_value, gelu_slope)


def swap(blocks, axes):
    return lax.all_to_all(blocks, axes, split_axis=0, concat_axis=0, tiled=True)


def spread(block, axes, size):
    copies = jnp.broadcast_to(block[None], (size,) + block.shape)
    return swap(copies.reshape((size * block.shape[0],) + block.shape[1:]), axes)


def gather(block, axis):
    return lax.all_gather(block, axis, axis=0, tiled=True)


def other(block, axis):
    return lax.ppermute(block, axis, [(0, 1), (1, 0)])


def per_device(inputs, w_up, w_down, grad_out):
    f32, bf16 = jnp.float32, jnp.bfloat16
    tokens, width = inputs.shape
    hidden = w_up.shape[1]
    xl, xh, core = lax.axis_index("xl"), lax.axis_index("xh"), lax.axis_index("c")

    def over_cores(part):
        part = gather(part, "c").reshape(16, 2, tokens, width)
        return part[:, 0].reshape(-1, width), part[:, 1].reshape(-1, width)

    def half(rows, which):
        size = rows.shape[0] // 2
        return lax.dynamic_slice_in_dim(rows, which * size, size, 0)

    def pre_and_back(whole_in, whole_grad, which):
        return jnp.stack(
            [
                jnp.dot(half(whole_in, which), w_up, preferred_element_type=f32),
                lax.dot_general(
                    half(whole_grad, which),
                    w_down,
                    (((1,), (1,)), ((), ())),
                    preferred_element_type=f32,
                ),
            ]
        )

    def pair_sums(whole_in, whole_grad):
        got = other(pre_and_back(whole_in, whole_grad, 1 - xl).astype(bf16), "xl")
        sums = pre_and_back(whole_in, whole_grad, xl) + got.astype(f32)
        return sums.astype(bf16).reshape(2, 8, tokens, hidden)

    both = jnp.stack([inputs, grad_out])
    near = swap(jnp.broadcast_to(both[None], (8,) + both.shape).reshape(-1, width), "z")
    far = other(near, "xh")
    near_in, near_grad = over_cores(near)
    far_in, far_grad = over_cores(far)
    near_pairs = pair_sums(near_in, near_grad)
    far_pairs = pair_sums(far_in, far_grad)
    pairs = jnp.stack([near_pairs, far_pairs], axis=1).transpose(2, 0, 1, 3, 4)
    pieces = swap(pairs.reshape(-1, hidden), "y").reshape(8, 2, 2 * tokens, hidden)
    pre, back = jnp.sum(pieces.astype(f32), axis=0)

    gelu_value, gelu_slope = gelu_parts(pre)
    dpre = spread((back * gelu_slope).astype(bf16), ("xl", "y"), 16)
    dpre, act_rows = lax.optimization_barrier((dpre, gelu_value.astype(bf16)))
    act_mine = spread(act_rows, "y", 8)

    def in_of(which):
        rows = half(dpre, which).reshape(8, 2, tokens, hidden)
        rows = jnp.where(xh == 0, rows, rows[:, ::-1])
        return lax.dot_general(
            jnp.swapaxes(rows, 0, 1).reshape(-1, hidden),
            w_up,
            (((1,), (1,)), ((), ())),
            preferred_element_type=f32,
        )

    def got_from(given):
        both = gather(given, "c")
        return half(both, 1 - core)

    given, kept = in_of(1 - core), in_of(core)
    size = given.shape[0] // 2
    got = jnp.concatenate([got_from(given[:size]), got_from(given[size:])])
    kept = (kept + got).astype(bf16)
    kept, act_mine = lax.optimization_barrier((kept, act_mine))
    pieces = swap(kept, ("xh", "z")).reshape(16, tokens, width)
    grad_in = jnp.sum(pieces.astype(f32), axis=0).astype(bf16)
    act_other = other(act_mine, "xl")

    def by_half(near, far):
        rows = [x.reshape(2, 8, tokens, width) for x in (near, far)]
        rows = jnp.stack(rows, axis=2).reshape(2, -1, width)
        return (
            lax.dynamic_index_in_dim(rows, xl, 0, False),
            lax.dynamic_index_in_dim(rows, 1 - xl, 0, False),
        )

    def over_tokens(left, right):
        return lax.dot_general(
            left, right, (((0,), (0,)), ((), ())), preferred_element_type=f32
        )

    def rows_of(near, far):
        parts = [x.reshape(16, tokens, width) for x in (near, far)]
        return jnp.stack(parts, axis=1).reshape(-1, width)

    grad_mine, grad_other = by_half(near_grad, far_grad)
    grad_up = over_tokens(rows_of(near_in, far_in), dpre)
    grad_down = over_tokens(act_mine, grad_mine) + over_tokens(act_other, grad_other)
    return (grad_in, grad_up.astype(bf16), grad_down.astype(bf16))


def solution(mesh):
    fine = Mesh(mesh.devices.reshape(2, 8, 8, 2, 2), ("xl", "y", "z", "xh", "c"))
    row, col = ("xl", "y"), ("z", "xh", "c")
    in_specs = (P(col, row), P(row, col), P(col, row), P(col, row))
    out_specs = (P(col, row), P(row, col), P(col, row))
    return jax.shard_map(
        per_device, mesh=fine, in_specs=in_specs, out_specs=out_specs, check_vma=False
    )
```

```python
import math

import jax
import jax.numpy as jnp
from jax import lax
from jax.sharding import Mesh, PartitionSpec as P

gelu_scale = math.sqrt(2.0 / math.pi)
cubic_coef = 0.044715


def gelu_parts(pre_act):
    tangent = jnp.tanh(gelu_scale * (pre_act + cubic_coef * pre_act * pre_act * pre_act))
    gelu_value = 0.5 * pre_act * (1.0 + tangent)
    gelu_slope = 0.5 * (1.0 + tangent) + 0.5 * pre_act * (1.0 - tangent * tangent) * gelu_scale * (
        1.0 + 3.0 * cubic_coef * pre_act * pre_act
    )
    return (gelu_value, gelu_slope)


def swap(blocks, axes):
    return lax.all_to_all(blocks, axes, split_axis=0, concat_axis=0, tiled=True)


def spread(block, axes, size):
    copies = jnp.broadcast_to(block[None], (size,) + block.shape)
    return swap(copies.reshape((size * block.shape[0],) + block.shape[1:]), axes)


def gather(block, axis):
    return lax.all_gather(block, axis, axis=0, tiled=True)


def other(block, axis):
    return lax.ppermute(block, axis, [(0, 1), (1, 0)])


def per_device(inputs, w_up, w_down, grad_out):
    f32, bf16 = jnp.float32, jnp.bfloat16
    tokens, width = inputs.shape
    hidden = w_up.shape[1]
    xl, xh, core = lax.axis_index("xl"), lax.axis_index("xh"), lax.axis_index("c")

    def over_cores(part):
        part = gather(part, "c").reshape(16, 2, tokens, width)
        return part[:, 0].reshape(-1, width), part[:, 1].reshape(-1, width)

    def half(rows, which):
        size = rows.shape[0] // 2
        return lax.dynamic_slice_in_dim(rows, which * size, size, 0)

    def pre_and_back(whole_in, whole_grad, which):
        return jnp.stack(
            [
                jnp.dot(half(whole_in, which), w_up, preferred_element_type=f32),
                lax.dot_general(
                    half(whole_grad, which),
                    w_down,
                    (((1,), (1,)), ((), ())),
                    preferred_element_type=f32,
                ),
            ]
        )

    def pair_sums(whole_in, whole_grad):
        got = other(pre_and_back(whole_in, whole_grad, 1 - xl).astype(bf16), "xl")
        sums = pre_and_back(whole_in, whole_grad, xl) + got.astype(f32)
        return sums.astype(bf16).reshape(2, 8, tokens, hidden)

    both = jnp.stack([inputs, grad_out])
    near = swap(jnp.broadcast_to(both[None], (8,) + both.shape).reshape(-1, width), "z")
    far = other(near, "xh")
    near_in, near_grad = over_cores(near)
    far_in, far_grad = over_cores(far)
    near_pairs = pair_sums(near_in, near_grad)
    far_pairs = pair_sums(far_in, far_grad)
    pairs = jnp.stack([near_pairs, far_pairs], axis=1).transpose(2, 0, 1, 3, 4)
    pieces = swap(pairs.reshape(-1, hidden), "y").reshape(8, 2, 2 * tokens, hidden)
    pre, back = jnp.sum(pieces.astype(f32), axis=0)

    gelu_value, gelu_slope = gelu_parts(pre)
    dpre = spread((back * gelu_slope).astype(bf16), ("xl", "y"), 16)
    dpre, act_rows = lax.optimization_barrier((dpre, gelu_value.astype(bf16)))
    act_mine = spread(act_rows, "y", 8)
    act_other = other(act_mine, "xl")

    def in_of(which):
        rows = half(dpre, which).reshape(8, 2, tokens, hidden)
        rows = jnp.where(xh == 0, rows, rows[:, ::-1])
        return lax.dot_general(
            jnp.swapaxes(rows, 0, 1).reshape(-1, hidden),
            w_up,
            (((1,), (1,)), ((), ())),
            preferred_element_type=f32,
        )

    def got_from(given):
        both = gather(given, "c")
        return half(both, 1 - core)

    given, kept = in_of(1 - core), in_of(core)
    size = given.shape[0] // 2
    got = jnp.concatenate([got_from(given[:size]), got_from(given[size:])])
    kept = (kept + got).astype(bf16)
    kept, act_mine = lax.optimization_barrier((kept, act_mine))
    pieces = swap(kept, ("xh", "z")).reshape(16, tokens, width)
    grad_in = jnp.sum(pieces.astype(f32), axis=0).astype(bf16)
    def by_half(near, far):
        rows = [x.reshape(2, 8, tokens, width) for x in (near, far)]
        rows = jnp.stack(rows, axis=2).reshape(2, -1, width)
        return (
            lax.dynamic_index_in_dim(rows, xl, 0, False),
            lax.dynamic_index_in_dim(rows, 1 - xl, 0, False),
        )

    def over_tokens(left, right):
        return lax.dot_general(
            left, right, (((0,), (0,)), ((), ())), preferred_element_type=f32
        )

    def rows_of(near, far):
        parts = [x.reshape(16, tokens, width) for x in (near, far)]
        return jnp.stack(parts, axis=1).reshape(-1, width)

    grad_mine, grad_other = by_half(near_grad, far_grad)
    grad_up = over_tokens(rows_of(near_in, far_in), dpre)
    grad_down = over_tokens(act_mine, grad_mine) + over_tokens(act_other, grad_other)
    return (grad_in, grad_up.astype(bf16), grad_down.astype(bf16))


def solution(mesh):
    fine = Mesh(mesh.devices.reshape(2, 8, 8, 2, 2), ("xl", "y", "z", "xh", "c"))
    row, col = ("xl", "y"), ("z", "xh", "c")
    in_specs = (P(col, row), P(row, col), P(col, row), P(col, row))
    out_specs = (P(col, row), P(row, col), P(col, row))
    return jax.shard_map(
        per_device, mesh=fine, in_specs=in_specs, out_specs=out_specs, check_vma=False
    )
```

```python
import math

import jax
import jax.numpy as jnp
from jax import lax
from jax.sharding import Mesh, PartitionSpec as P

gelu_scale = math.sqrt(2.0 / math.pi)
cubic_coef = 0.044715


def gelu_parts(pre_act):
    tangent = jnp.tanh(gelu_scale * (pre_act + cubic_coef * pre_act * pre_act * pre_act))
    gelu_value = 0.5 * pre_act * (1.0 + tangent)
    gelu_slope = 0.5 * (1.0 + tangent) + 0.5 * pre_act * (1.0 - tangent * tangent) * gelu_scale * (
        1.0 + 3.0 * cubic_coef * pre_act * pre_act
    )
    return (gelu_value, gelu_slope)


def swap(blocks, axes):
    return lax.all_to_all(blocks, axes, split_axis=0, concat_axis=0, tiled=True)


def spread(block, axes, size):
    copies = jnp.broadcast_to(block[None], (size,) + block.shape)
    return swap(copies.reshape((size * block.shape[0],) + block.shape[1:]), axes)


def gather(block, axis):
    return lax.all_gather(block, axis, axis=0, tiled=True)


def other(block, axis):
    return lax.ppermute(block, axis, [(0, 1), (1, 0)])


def per_device(inputs, w_up, w_down, grad_out):
    f32, bf16 = jnp.float32, jnp.bfloat16
    tokens, width = inputs.shape
    hidden = w_up.shape[1]
    xl, xh, core = lax.axis_index("xl"), lax.axis_index("xh"), lax.axis_index("c")

    def over_cores(part):
        part = gather(part, "c").reshape(16, 2, tokens, width)
        return part[:, 0].reshape(-1, width), part[:, 1].reshape(-1, width)

    def half(rows, which):
        size = rows.shape[0] // 2
        return lax.dynamic_slice_in_dim(rows, which * size, size, 0)

    def pre_and_back(whole_in, whole_grad, which):
        return jnp.stack(
            [
                jnp.dot(half(whole_in, which), w_up, preferred_element_type=f32),
                lax.dot_general(
                    half(whole_grad, which),
                    w_down,
                    (((1,), (1,)), ((), ())),
                    preferred_element_type=f32,
                ),
            ]
        )

    def pair_sums(whole_in, whole_grad):
        got = other(pre_and_back(whole_in, whole_grad, 1 - xl).astype(bf16), "xl")
        sums = pre_and_back(whole_in, whole_grad, xl) + got.astype(f32)
        return sums.astype(bf16).reshape(2, 8, tokens, hidden)

    both = jnp.stack([inputs, grad_out])
    near = swap(jnp.broadcast_to(both[None], (8,) + both.shape).reshape(-1, width), "z")
    far = other(near, "xh")
    near_in, near_grad = over_cores(near)
    far_in, far_grad = over_cores(far)
    near_pairs = pair_sums(near_in, near_grad)
    far_pairs = pair_sums(far_in, far_grad)
    pairs = jnp.stack([near_pairs, far_pairs], axis=1).transpose(2, 0, 1, 3, 4)
    pieces = swap(pairs.reshape(-1, hidden), "y").reshape(8, 2, 2 * tokens, hidden)
    pre, back = jnp.sum(pieces.astype(f32), axis=0)

    gelu_value, gelu_slope = gelu_parts(pre)
    dpre = spread((back * gelu_slope).astype(bf16), ("xl", "y"), 16)
    act_rows = gelu_value.astype(bf16)
    act_copies = jnp.broadcast_to(act_rows[None], (8,) + act_rows.shape)
    dpre, act_copies = lax.optimization_barrier((dpre, act_copies))
    act_mine = swap(act_copies.reshape(-1, hidden), "y")
    act_other = other(act_mine, "xl")

    def in_of(which):
        rows = half(dpre, which).reshape(8, 2, tokens, hidden)
        rows = jnp.where(xh == 0, rows, rows[:, ::-1])
        return lax.dot_general(
            jnp.swapaxes(rows, 0, 1).reshape(-1, hidden),
            w_up,
            (((1,), (1,)), ((), ())),
            preferred_element_type=f32,
        )

    def got_from(given):
        both = gather(given, "c")
        return half(both, 1 - core)

    given, kept = in_of(1 - core), in_of(core)
    size = given.shape[0] // 2
    got = jnp.concatenate([got_from(given[:size]), got_from(given[size:])])
    kept = (kept + got).astype(bf16)
    kept, act_mine = lax.optimization_barrier((kept, act_mine))
    pieces = swap(kept, ("xh", "z")).reshape(16, tokens, width)
    grad_in = jnp.sum(pieces.astype(f32), axis=0).astype(bf16)
    def by_half(near, far):
        rows = [x.reshape(2, 8, tokens, width) for x in (near, far)]
        rows = jnp.stack(rows, axis=2).reshape(2, -1, width)
        return (
            lax.dynamic_index_in_dim(rows, xl, 0, False),
            lax.dynamic_index_in_dim(rows, 1 - xl, 0, False),
        )

    def over_tokens(left, right):
        return lax.dot_general(
            left, right, (((0,), (0,)), ((), ())), preferred_element_type=f32
        )

    def rows_of(near, far):
        parts = [x.reshape(16, tokens, width) for x in (near, far)]
        return jnp.stack(parts, axis=1).reshape(-1, width)

    grad_mine, grad_other = by_half(near_grad, far_grad)
    grad_up = over_tokens(rows_of(near_in, far_in), dpre)
    grad_down = over_tokens(act_mine, grad_mine) + over_tokens(act_other, grad_other)
    return (grad_in, grad_up.astype(bf16), grad_down.astype(bf16))


def solution(mesh):
    fine = Mesh(mesh.devices.reshape(2, 8, 8, 2, 2), ("xl", "y", "z", "xh", "c"))
    row, col = ("xl", "y"), ("z", "xh", "c")
    in_specs = (P(col, row), P(row, col), P(col, row), P(col, row))
    out_specs = (P(col, row), P(row, col), P(col, row))
    return jax.shard_map(
        per_device, mesh=fine, in_specs=in_specs, out_specs=out_specs, check_vma=False
    )
```

```python
import math

import jax
import jax.numpy as jnp
from jax import lax
from jax.sharding import Mesh, PartitionSpec as P

gelu_scale = math.sqrt(2.0 / math.pi)
cubic_coef = 0.044715


def gelu_parts(pre_act):
    tangent = jnp.tanh(gelu_scale * (pre_act + cubic_coef * pre_act * pre_act * pre_act))
    gelu_value = 0.5 * pre_act * (1.0 + tangent)
    gelu_slope = 0.5 * (1.0 + tangent) + 0.5 * pre_act * (1.0 - tangent * tangent) * gelu_scale * (
        1.0 + 3.0 * cubic_coef * pre_act * pre_act
    )
    return (gelu_value, gelu_slope)


def swap(blocks, axes):
    return lax.all_to_all(blocks, axes, split_axis=0, concat_axis=0, tiled=True)


def spread(block, axes, size):
    copies = jnp.broadcast_to(block[None], (size,) + block.shape)
    return swap(copies.reshape((size * block.shape[0],) + block.shape[1:]), axes)


def gather(block, axis):
    return lax.all_gather(block, axis, axis=0, tiled=True)


def other(block, axis):
    return lax.ppermute(block, axis, [(0, 1), (1, 0)])


def per_device(inputs, w_up, w_down, grad_out):
    f32, bf16 = jnp.float32, jnp.bfloat16
    tokens, width = inputs.shape
    hidden = w_up.shape[1]
    xl, xh, core = lax.axis_index("xl"), lax.axis_index("xh"), lax.axis_index("c")

    def over_cores(part):
        part = gather(part, "c").reshape(16, 2, tokens, width)
        return part[:, 0].reshape(-1, width), part[:, 1].reshape(-1, width)

    def half(rows, which):
        size = rows.shape[0] // 2
        return lax.dynamic_slice_in_dim(rows, which * size, size, 0)

    def pre_and_back(whole_in, whole_grad, which):
        return jnp.stack(
            [
                jnp.dot(half(whole_in, which), w_up, preferred_element_type=f32),
                lax.dot_general(
                    half(whole_grad, which),
                    w_down,
                    (((1,), (1,)), ((), ())),
                    preferred_element_type=f32,
                ),
            ]
        )

    def pair_sums(whole_in, whole_grad):
        got = other(pre_and_back(whole_in, whole_grad, 1 - xl).astype(bf16), "xl")
        sums = pre_and_back(whole_in, whole_grad, xl) + got.astype(f32)
        return sums.astype(bf16).reshape(2, 8, tokens, hidden)

    which = lax.broadcasted_iota(jnp.int32, (8, 2, tokens, width), 1)
    both = jnp.where(which == 0, inputs[None, None], grad_out[None, None])
    near = swap(both.reshape(-1, width), "z")
    far = other(near, "xh")
    near_in, near_grad = over_cores(near)
    far_in, far_grad = over_cores(far)
    near_pairs = pair_sums(near_in, near_grad)
    far_pairs = pair_sums(far_in, far_grad)
    pairs = jnp.stack([near_pairs, far_pairs], axis=1).transpose(2, 0, 1, 3, 4)
    pieces = swap(pairs.reshape(-1, hidden), "y").reshape(8, 2, 2 * tokens, hidden)
    pre, back = jnp.sum(pieces.astype(f32), axis=0)

    gelu_value, gelu_slope = gelu_parts(pre)
    dpre = spread((back * gelu_slope).astype(bf16), ("xl", "y"), 16)
    act_rows = gelu_value.astype(bf16)
    act_copies = jnp.broadcast_to(act_rows[None], (8,) + act_rows.shape)
    dpre, act_copies = lax.optimization_barrier((dpre, act_copies))
    act_mine = swap(act_copies.reshape(-1, hidden), "y")
    act_other = other(act_mine, "xl")

    def in_of(which):
        rows = half(dpre, which).reshape(8, 2, tokens, hidden)
        rows = jnp.where(xh == 0, rows, rows[:, ::-1])
        return lax.dot_general(
            jnp.swapaxes(rows, 0, 1).reshape(-1, hidden),
            w_up,
            (((1,), (1,)), ((), ())),
            preferred_element_type=f32,
        )

    def got_from(given):
        both = gather(given, "c")
        return half(both, 1 - core)

    given, kept = in_of(1 - core), in_of(core)
    size = given.shape[0] // 2
    got = jnp.concatenate([got_from(given[:size]), got_from(given[size:])])
    kept = (kept + got).astype(bf16)
    kept, act_mine = lax.optimization_barrier((kept, act_mine))
    pieces = swap(kept, ("xh", "z")).reshape(16, tokens, width)
    grad_in = jnp.sum(pieces.astype(f32), axis=0).astype(bf16)
    def by_half(near, far):
        rows = [x.reshape(2, 8, tokens, width) for x in (near, far)]
        rows = jnp.stack(rows, axis=2).reshape(2, -1, width)
        return (
            lax.dynamic_index_in_dim(rows, xl, 0, False),
            lax.dynamic_index_in_dim(rows, 1 - xl, 0, False),
        )

    def over_tokens(left, right):
        return lax.dot_general(
            left, right, (((0,), (0,)), ((), ())), preferred_element_type=f32
        )

    def rows_of(near, far):
        parts = [x.reshape(16, tokens, width) for x in (near, far)]
        return jnp.stack(parts, axis=1).reshape(-1, width)

    grad_mine, grad_other = by_half(near_grad, far_grad)
    grad_up = over_tokens(rows_of(near_in, far_in), dpre)
    grad_down = over_tokens(act_mine, grad_mine) + over_tokens(act_other, grad_other)
    return (grad_in, grad_up.astype(bf16), grad_down.astype(bf16))


def solution(mesh):
    fine = Mesh(mesh.devices.reshape(2, 8, 8, 2, 2), ("xl", "y", "z", "xh", "c"))
    row, col = ("xl", "y"), ("z", "xh", "c")
    in_specs = (P(col, row), P(row, col), P(col, row), P(col, row))
    out_specs = (P(col, row), P(row, col), P(col, row))
    return jax.shard_map(
        per_device, mesh=fine, in_specs=in_specs, out_specs=out_specs, check_vma=False
    )
```

```python
import math

import jax
import jax.numpy as jnp
from jax import lax
from jax.sharding import Mesh, PartitionSpec as P

gelu_scale = math.sqrt(2.0 / math.pi)
cubic_coef = 0.044715


def gelu_parts(pre_act):
    tangent = jnp.tanh(gelu_scale * (pre_act + cubic_coef * pre_act * pre_act * pre_act))
    gelu_value = 0.5 * pre_act * (1.0 + tangent)
    gelu_slope = 0.5 * (1.0 + tangent) + 0.5 * pre_act * (1.0 - tangent * tangent) * gelu_scale * (
        1.0 + 3.0 * cubic_coef * pre_act * pre_act
    )
    return (gelu_value, gelu_slope)


def swap(blocks, axes):
    return lax.all_to_all(blocks, axes, split_axis=0, concat_axis=0, tiled=True)


def spread(block, axes, size):
    copies = jnp.broadcast_to(block[None], (size,) + block.shape)
    return swap(copies.reshape((size * block.shape[0],) + block.shape[1:]), axes)


def gather(block, axis):
    return lax.all_gather(block, axis, axis=0, tiled=True)


def other(block, axis):
    return lax.ppermute(block, axis, [(0, 1), (1, 0)])


def per_device(inputs, w_up, w_down, grad_out):
    f32, bf16 = jnp.float32, jnp.bfloat16
    tokens, width = inputs.shape
    hidden = w_up.shape[1]
    xl, xh, core = lax.axis_index("xl"), lax.axis_index("xh"), lax.axis_index("c")

    def over_cores(part):
        part = gather(part, "c").reshape(16, 2, tokens, width)
        return part[:, 0].reshape(-1, width), part[:, 1].reshape(-1, width)

    def half(rows, which):
        size = rows.shape[0] // 2
        return lax.dynamic_slice_in_dim(rows, which * size, size, 0)

    def pre_and_back(whole_in, whole_grad, which):
        return jnp.stack(
            [
                jnp.dot(half(whole_in, which), w_up, preferred_element_type=f32),
                lax.dot_general(
                    half(whole_grad, which),
                    w_down,
                    (((1,), (1,)), ((), ())),
                    preferred_element_type=f32,
                ),
            ]
        )

    def pair_sums(whole_in, whole_grad):
        got = other(pre_and_back(whole_in, whole_grad, 1 - xl).astype(bf16), "xl")
        sums = pre_and_back(whole_in, whole_grad, xl) + got.astype(f32)
        return sums.astype(bf16).reshape(2, 8, tokens, hidden)

    both = jnp.stack([inputs, grad_out])
    near = swap(jnp.broadcast_to(both[None], (8,) + both.shape).reshape(-1, width), "z")
    far = other(near, "xh")
    near_in, near_grad = over_cores(near)
    far_in, far_grad = over_cores(far)
    near_pairs = pair_sums(near_in, near_grad)
    far_pairs = pair_sums(far_in, far_grad)
    pairs = jnp.stack([near_pairs, far_pairs], axis=1).transpose(2, 0, 1, 3, 4)
    pieces = swap(pairs.reshape(-1, hidden), "y").reshape(8, 2, 2 * tokens, hidden)
    pre, back = jnp.sum(pieces.astype(f32), axis=0)

    gelu_value, gelu_slope = gelu_parts(pre)
    dpre = spread((back * gelu_slope).astype(bf16), ("xl", "y"), 16)
    act_rows = gelu_value.astype(bf16)
    act_copies = jnp.broadcast_to(act_rows[None], (8,) + act_rows.shape)
    dpre, act_copies = lax.optimization_barrier((dpre, act_copies))
    act_mine = swap(act_copies.reshape(-1, hidden), "y")
    act_other = other(act_mine, "xl")

    def in_of(which):
        rows = half(dpre, which).reshape(8, 2, tokens, hidden)
        rows = jnp.where(xh == 0, rows, rows[:, ::-1])
        return lax.dot_general(
            jnp.swapaxes(rows, 0, 1).reshape(-1, hidden),
            w_up,
            (((1,), (1,)), ((), ())),
            preferred_element_type=f32,
        )

    def got_from(given):
        both = gather(given, "c")
        return half(both, 1 - core)

    given, kept = in_of(1 - core), in_of(core)
    got = got_from(given.astype(bf16)).astype(f32)
    kept = (kept + got).astype(bf16)
    kept, act_mine = lax.optimization_barrier((kept, act_mine))
    pieces = swap(kept, ("xh", "z")).reshape(16, tokens, width)
    grad_in = jnp.sum(pieces.astype(f32), axis=0).astype(bf16)
    def by_half(near, far):
        rows = [x.reshape(2, 8, tokens, width) for x in (near, far)]
        rows = jnp.stack(rows, axis=2).reshape(2, -1, width)
        return (
            lax.dynamic_index_in_dim(rows, xl, 0, False),
            lax.dynamic_index_in_dim(rows, 1 - xl, 0, False),
        )

    def over_tokens(left, right):
        return lax.dot_general(
            left, right, (((0,), (0,)), ((), ())), preferred_element_type=f32
        )

    def rows_of(near, far):
        parts = [x.reshape(16, tokens, width) for x in (near, far)]
        return jnp.stack(parts, axis=1).reshape(-1, width)

    grad_mine, grad_other = by_half(near_grad, far_grad)
    grad_up = over_tokens(rows_of(near_in, far_in), dpre)
    grad_down = over_tokens(act_mine, grad_mine) + over_tokens(act_other, grad_other)
    return (grad_in, grad_up.astype(bf16), grad_down.astype(bf16))


def solution(mesh):
    fine = Mesh(mesh.devices.reshape(2, 8, 8, 2, 2), ("xl", "y", "z", "xh", "c"))
    row, col = ("xl", "y"), ("z", "xh", "c")
    in_specs = (P(col, row), P(row, col), P(col, row), P(col, row))
    out_specs = (P(col, row), P(row, col), P(col, row))
    return jax.shard_map(
        per_device, mesh=fine, in_specs=in_specs, out_specs=out_specs, check_vma=False
    )
```
